32 devices in a mesh: fsdp: 16 (over z, y, x), seq: 2 (over core).
Axes of the slice: x: 2, y: 2, z: 4, core: 2. Of those that a mesh axis runs over, the one named last changes fastest.
Arguments:
- latents: bfloat16 [16, 1024, 1152], P('fsdp', 'seq'), may hold values from -3 to 3
- captions: bfloat16 [16, 120, 1152], P('fsdp'), may hold values from -3 to 3
- conditions: float32 [16, 6912], P('fsdp'), may hold values from -0.75 to 0.75
- table: bfloat16 [6, 1152], P(None, 'fsdp'), may hold values from -0.75 to 0.75
- w_qkv: bfloat16 [1152, 3456], P('fsdp'), may hold values from -0.1875 to 0.1875
- w_out: bfloat16 [1152, 1152], P('fsdp'), may hold values from -1.5 to 1.5
- w_cross_q: bfloat16 [1152, 1152], P('fsdp'), may hold values from -0.1875 to 0.1875
- w_cross_kv: bfloat16 [1152, 2304], P('fsdp'), may hold values from -0.1875 to 0.1875
- w_cross_out: bfloat16 [1152, 1152], P('fsdp'), may hold values from -0.5 to 0.5
- w_fc_in: bfloat16 [1152, 4608], P('fsdp'), may hold values from -0.1875 to 0.1875
- w_fc_out: bfloat16 [4608, 1152], P('fsdp'), may hold values from -0.09375 to 0.09375
- cotangent: bfloat16 [16, 1024, 1152], P('fsdp', 'seq'), may hold values from -3 to 3
Outputs:
- output: bfloat16 [16, 1024, 1152], P('fsdp', 'seq')
- grad_latents: float32 [16, 1024, 1152], P('fsdp', 'seq')
- grad_captions: float32 [16, 120, 1152], P('fsdp')
- grad_conditions: float32 [16, 6912], P('fsdp')
- grad_mlp_shift: float32 [16, 1152], P('fsdp')
- grad_table: float32 [6, 1152], P(None, 'fsdp')
- grad_w_qkv: float32 [1152, 3456], P('fsdp')
- grad_w_out: float32 [1152, 1152], P('fsdp')
- grad_w_cross_q: float32 [1152, 1152], P('fsdp')
- grad_w_cross_kv: float32 [1152, 2304], P('fsdp')
- grad_w_cross_out: float32 [1152, 1152], P('fsdp')
- grad_w_fc_in: float32 [1152, 4608], P('fsdp')
- grad_w_fc_out: float32 [4608, 1152], P('fsdp')
The draws below stay inside these ranges and needn't reach their ends.
All inputs are finite; a program needn't handle non-finite values.
Results may differ from the reference program's by a relative error of at most 0.03.
Values may be sent and summed in bfloat16 or wider, within the bound.
A program may use at most 224 MiB of HBM per device.

```python
import math
import jax
import jax.numpy as jnp
from jax import lax

H = 16
HD = 72
FF = 4608
D = 1152
TXT = 120
LEN = 1024
SEQS = 16


def shard_levels(stream_key, shape, cuts, low, top_value):
    loudness = 1.0
    for dim, parts in cuts:
        heights = jax.random.uniform(jax.random.fold_in(jax.random.fold_in(stream_key, 6), dim), (parts,), jnp.float32, low / len(cuts), top_value / len(cuts))
        loudness = loudness * jnp.repeat(jnp.exp(heights), shape[dim] // parts).reshape((-1,) + (1,) * (len(shape) - 1 - dim))
    return loudness


def noise(stream_key, dims, width, bound, pieces=(), dtype=jnp.bfloat16):
    factor_of = shard_levels(stream_key, dims, pieces, -0.22, 0.18) if pieces else 1.0
    result = jax.random.normal(stream_key, dims, jnp.float32) * width * factor_of
    return jnp.minimum(jnp.maximum(result, -bound), bound).astype(dtype)


def setup_inputs(seed: int = 0) -> dict:
    key_of = jax.random.split(jax.random.key(seed), 13)
    latents = noise(key_of[0], (SEQS, LEN, D), 1.0, 3.0, ((0, 16), (1, 2)))
    captions = noise(key_of[1], (SEQS, TXT, D), 1.0, 3.0, ((0, 16),))
    conditions = noise(key_of[2], (SEQS, 6 * D), 0.3, 0.75, ((0, 16),), jnp.float32)
    table = noise(key_of[3], (6, D), 0.3, 0.75, ((1, 16),))
    w_qkv = noise(key_of[4], (D, 3 * D), D ** -0.5, 0.1875, ((0, 16),))
    w_out = noise(key_of[5], (D, D), (D * 16 // LEN) ** -0.5, 1.5, ((0, 16),))
    w_cross_q = noise(key_of[6], (D, D), D ** -0.5, 0.1875, ((0, 16),))
    w_cross_kv = noise(key_of[7], (D, 2 * D), D ** -0.5, 0.1875, ((0, 16),))
    w_cross_out = noise(key_of[8], (D, D), (D * 16 // TXT) ** -0.5, 0.5, ((0, 16),))
    w_fc_in = noise(key_of[9], (D, FF), D ** -0.5, 0.1875, ((0, 16),))
    w_fc_out = noise(key_of[10], (FF, D), FF ** -0.5, 0.09375, ((0, 16),))
    cotangent = noise(key_of[11], (SEQS, LEN, D), 1.0, 3.0, ((0, 16), (1, 2)))
    return dict(latents=latents, captions=captions, conditions=conditions, table=table, w_qkv=w_qkv, w_out=w_out, w_cross_q=w_cross_q, w_cross_kv=w_cross_kv, w_cross_out=w_cross_out, w_fc_in=w_fc_in, w_fc_out=w_fc_out, cotangent=cotangent)


@jax.custom_vjp
def low(v):
    return lax.optimization_barrier(v.astype(jnp.bfloat16)).astype(jnp.float32)

@jax.custom_vjp
def low_back(v):
    return v

def low_keep(v):
    return (low(v), None)

def low_pass(kept, grad):
    return (grad,)

def back_keep(v):
    return (v, None)

def back_low(kept, grad):
    return (low(grad),)
low.defvjp(low_keep, low_pass)
low_back.defvjp(back_keep, back_low)
eps_norm = 1e-06

def matmul(left_side, right_side):
    return jnp.dot(left_side, right_side, precision=lax.Precision.HIGHEST)

def layer_norm(values):
    average = lax.optimization_barrier(jnp.mean(values, axis=-1, keepdims=True))
    centred = values - average
    variance = lax.optimization_barrier(jnp.mean(centred * centred, axis=-1, keepdims=True))
    return centred * lax.rsqrt(variance + eps_norm)

def attend(queries, key_rows, value_rows):
    split_q = queries.reshape(queries.shape[0], H, HD)
    split_k = key_rows.reshape(key_rows.shape[0], H, HD)
    split_v = value_rows.reshape(value_rows.shape[0], H, HD)
    scores = low_back(jnp.einsum('qhd,khd->hqk', split_q, split_k, precision=lax.Precision.HIGHEST) * (1.0 / math.sqrt(HD)))
    probability = low(jax.nn.softmax(scores, axis=-1))
    mixed_rows = jnp.einsum('hqk,khd->qhd', probability, split_v, precision=lax.Precision.HIGHEST)
    return low(low_back(mixed_rows.reshape(queries.shape[0], H * HD)))

def one_sequence(latent, caption, condition, weights):
    table, w_qkv, w_out, w_cross_q, w_cross_kv, w_cross_out, w_fc_in, w_fc_out = weights
    modulation = table + condition.reshape(6, D)
    shift_one, scale_one, gate_one, shift_two, scale_two, gate_two = modulation
    normed = low(layer_norm(latent) * (1.0 + scale_one) + shift_one)
    joined = low(low_back(matmul(normed, w_qkv)))
    mixed_self = attend(joined[:, :D], joined[:, D:2 * D], joined[:, 2 * D:])
    branch = low_back(matmul(mixed_self, w_out))
    after_self = latent + gate_one * branch
    cross_in = low(after_self)
    cross_query = low(low_back(matmul(cross_in, w_cross_q)))
    cross_kv = low(low_back(matmul(caption, w_cross_kv)))
    cross_mixed = attend(cross_query, cross_kv[:, :D], cross_kv[:, D:])
    after_cross = after_self + low_back(matmul(cross_mixed, w_cross_out))
    normed_two = low(layer_norm(after_cross) * (1.0 + scale_two) + shift_two)
    hidden_pre = low_back(matmul(normed_two, w_fc_in))
    hidden = low(jax.nn.gelu(hidden_pre, approximate=True))
    return after_cross + gate_two * low_back(matmul(hidden, w_fc_out))

def reference(latents, captions, conditions, table, w_qkv, w_out, w_cross_q, w_cross_kv, w_cross_out, w_fc_in, w_fc_out, cotangent):
    weights = tuple((weight.astype(jnp.float32) for weight in (table, w_qkv, w_out, w_cross_q, w_cross_kv, w_cross_out, w_fc_in, w_fc_out)))

    def forward(latent_all, caption_all, condition_all, weight_all):

        def single(sequence_items):
            return jax.checkpoint(one_sequence)(sequence_items[0], sequence_items[1], sequence_items[2], weight_all)
        return lax.map(single, (latent_all, caption_all, condition_all))
    output, pullback = jax.vjp(forward, latents.astype(jnp.float32), captions.astype(jnp.float32), conditions, weights)
    grad_latents, grad_captions, grad_conditions, grad_weights = pullback(cotangent.astype(jnp.float32))
    grad_table, grad_w_qkv, grad_w_out, grad_w_cross_q, grad_w_cross_kv, grad_w_cross_out, grad_w_fc_in, grad_w_fc_out = grad_weights
    grad_mlp_shift = grad_conditions[:, 3 * D:4 * D]
    return (output.astype(jnp.bfloat16), grad_latents, grad_captions, grad_conditions, grad_mlp_shift, grad_table, grad_w_qkv, grad_w_out, grad_w_cross_q, grad_w_cross_kv, grad_w_cross_out, grad_w_fc_in, grad_w_fc_out)
```

```python
import math

import jax
import jax.numpy as jnp
from jax import lax
from jax.sharding import PartitionSpec as P

H = 16
HD = 72


eps_norm = 1e-06


def layer_norm(values):
    average = jnp.mean(values, axis=-1, keepdims=True)
    centred = values - average
    variance = jnp.mean(centred * centred, axis=-1, keepdims=True)
    return centred * lax.rsqrt(variance + eps_norm)


def modulate(values, shift_rows, scale_rows):
    return layer_norm(values) * (1.0 + scale_rows[:, None, :]) + shift_rows[:, None, :]


def gelu_tanh(values):
    return jax.nn.gelu(values, approximate=True)


def product(left_side, right_side):
    return jnp.dot(left_side, right_side, preferred_element_type=jnp.float32)


def outer_sum(left_side, right_side):
    return lax.dot_general(
        left_side, right_side, (((0,), (0,)), ((), ())), preferred_element_type=jnp.float32
    )


def back_product(left_side, right_side):
    return lax.dot_general(
        left_side, right_side, (((1,), (1,)), ((), ())), preferred_element_type=jnp.float32
    )


def split_heads(values):
    return values.reshape(values.shape[0], values.shape[1], H, HD)


def attention_scores(queries, key_rows):
    return jnp.einsum(
        "sqhd,skhd->shqk",
        split_heads(queries),
        split_heads(key_rows),
        preferred_element_type=jnp.float32,
    ) * (1.0 / math.sqrt(HD))


def attention_forward(queries, key_rows, value_rows):
    scores = attention_scores(queries, key_rows)
    row_max = jnp.max(scores, axis=-1, keepdims=True)
    exponent = jnp.exp(scores - row_max)
    denominator = jnp.sum(exponent, axis=-1, keepdims=True)
    probability = (exponent / denominator).astype(jnp.bfloat16)
    log_total = row_max + jnp.log(denominator)
    mixed_rows = jnp.einsum(
        "shqk,skhd->sqhd", probability, split_heads(value_rows), preferred_element_type=jnp.float32
    )
    return (mixed_rows.reshape(queries.shape).astype(jnp.bfloat16), log_total)


def score_grads(queries, key_rows, value_rows, log_total, grad_mixed, row_sums):
    probability = jnp.exp(attention_scores(queries, key_rows) - log_total)
    grad_prob = jnp.einsum(
        "sqhd,skhd->shqk",
        split_heads(grad_mixed),
        split_heads(value_rows),
        preferred_element_type=jnp.float32,
    )
    row_sums = jnp.sum(probability * grad_prob, axis=-1, keepdims=True)
    grad_scores = (probability * (grad_prob - row_sums)).astype(jnp.bfloat16)
    return (probability, grad_scores, row_sums)


def key_side(queries, key_rows, grad_mixed, probability, grad_scores):
    factor = 1.0 / math.sqrt(HD)
    grad_values = jnp.einsum(
        "shqk,sqhd->skhd",
        probability.astype(jnp.bfloat16),
        split_heads(grad_mixed),
        preferred_element_type=jnp.float32,
    )
    grad_keys = (
        jnp.einsum(
            "shqk,sqhd->skhd", grad_scores, split_heads(queries), preferred_element_type=jnp.float32
        )
        * factor
    )
    return (grad_keys.reshape(key_rows.shape), grad_values.reshape(key_rows.shape))


def query_side(key_rows, grad_scores, query_shape):
    factor = 1.0 / math.sqrt(HD)
    grad_queries = (
        jnp.einsum(
            "shqk,skhd->sqhd",
            grad_scores,
            split_heads(key_rows),
            preferred_element_type=jnp.float32,
        )
        * factor
    )
    return grad_queries.reshape(query_shape)


def attention_backward(queries, key_rows, value_rows, log_total, grad_mixed):
    probability, grad_scores, row_sums = score_grads(
        queries, key_rows, value_rows, log_total, grad_mixed, None
    )
    grad_queries = query_side(key_rows, grad_scores, queries.shape)
    grad_keys, grad_values = key_side(queries, key_rows, grad_mixed, probability, grad_scores)
    return (grad_queries, grad_keys, grad_values)

def bit_count(size):
    return size.bit_length() - 1


def swap(values, axis_name, bit):
    size = lax.axis_size(axis_name)
    return lax.ppermute(values, axis_name, [(i, i ^ (1 << bit)) for i in range(size)])


def my_bit(axis_name, bit):
    return lax.rem(lax.shift_right_logical(lax.axis_index(axis_name), jnp.int32(bit)), 2)


def exchange_gather(values, axis_name, rotation=0):
    bits = bit_count(lax.axis_size(axis_name))
    held = values.reshape((1,) * bits + values.shape)
    for step in range(bits):
        bit = (step + rotation) % bits
        dim = bits - 1 - bit
        other = swap(held, axis_name, bit)
        upper = my_bit(axis_name, bit) == 1
        held = jnp.concatenate(
            [jnp.where(upper, other, held), jnp.where(upper, held, other)], axis=dim
        )
    return held.reshape((1 << bits,) + values.shape)


def exchange_sum_scatter(values, axis_name, rotation=0, last=jnp.float32, lead=0):
    bits = bit_count(lax.axis_size(axis_name))
    held = values.reshape(values.shape[:lead] + (2,) * bits + values.shape[lead + 1 :])
    for step in range(bits):
        bit = (bits - 1 - step + rotation) % bits
        dim = lead + bits - 1 - bit
        mine = my_bit(axis_name, bit)
        kept = lax.dynamic_index_in_dim(held, mine, dim, keepdims=True)
        other = swap(lax.dynamic_index_in_dim(held, 1 - mine, dim, keepdims=True), axis_name, bit)
        total = kept.astype(jnp.float32) + other.astype(jnp.float32)
        held = total.astype(last if step == bits - 1 else values.dtype)
    return held.reshape(values.shape[:lead] + values.shape[lead + 1 :])


def exchange_sum(values, axis_name):
    for bit in range(bit_count(lax.axis_size(axis_name))):
        values = values + swap(values, axis_name, bit)
    return values


def column_units(shard, width):
    return [shard[:, i : i + width] for i in range(0, shard.shape[1], width)]


def gather_units(units, rotations):
    parts = lax.axis_size("seq")
    share = len(units) // parts
    stacked = jnp.stack(units).reshape((parts, share) + units[0].shape)
    mine = lax.dynamic_index_in_dim(stacked, lax.axis_index("seq"), 0, keepdims=False)
    gathered = jnp.stack(
        [
            exchange_gather(mine[i], "fsdp", rotations[i % len(rotations)])
            for i in range(share)
        ]
    )
    whole = exchange_gather(gathered, "seq")
    return whole.reshape((len(units), whole.shape[2]) + units[0].shape)


def scatter_units(units, rotations):
    parts = lax.axis_size("seq")
    share = len(units) // parts
    stacked = jnp.stack(units).reshape((parts, share) + units[0].shape)
    mine = exchange_sum_scatter(stacked, "seq", last=jnp.bfloat16)
    owned = jnp.stack(
        [
            exchange_sum_scatter(mine[i], "fsdp", rotations[i % len(rotations)])
            for i in range(share)
        ]
    )
    whole = exchange_gather(owned, "seq")
    return whole.reshape((len(units),) + units[0].shape[1:])


def grad_units(grad):
    width = grad.shape[0]
    low = grad.astype(jnp.bfloat16)
    devices = lax.axis_size("fsdp")
    return [
        piece.reshape(devices, width // devices, width) for piece in column_units(low, width)
    ]


ROTATIONS = ((0, 1), (2, 0), (1, 2), (0, 1))


def in_groups(function, units):
    size = max(4, lax.axis_size("seq"))
    results = []
    for number, start in enumerate(range(0, len(units), size)):
        group = function(units[start : start + size], ROTATIONS[number % len(ROTATIONS)])
        results.extend(group[i] for i in range(size))
    return results


def body(
    latents,
    captions,
    conditions,
    table,
    w_qkv,
    w_out,
    w_cross_q,
    w_cross_kv,
    w_cross_out,
    w_fc_in,
    w_fc_out,
    cotangent,
):
    width = latents.shape[-1]
    rows = w_out.shape[0]
    full_table = jnp.moveaxis(exchange_gather(table, "fsdp"), 0, 1).reshape(table.shape[0], width)
    whole_tiles = rows % 8 == 0
    if whole_tiles:
        pieces = in_groups(
            gather_units,
            column_units(w_qkv, width)
            + [w_out, w_cross_q]
            + column_units(w_cross_kv, width)
            + [w_cross_out]
            + column_units(w_fc_in, width)
            + [w_fc_out[i : i + rows] for i in range(0, w_fc_out.shape[0], rows)],
        )
        square = [piece.reshape(width, width) for piece in pieces[:12]]
        full_qkv = jnp.concatenate(square[0:3], axis=1)
        full_out, full_cq = square[3], square[4]
        full_ckv = jnp.concatenate(square[5:7], axis=1)
        full_co = square[7]
        full_fc_in = jnp.concatenate(square[8:12], axis=1)
        full_fc_out = jnp.stack(pieces[12:], axis=1).reshape(-1, width)
    else:
        full_qkv, full_out, full_cq, full_ckv, full_co, full_fc_in, full_fc_out = (
            lax.all_gather(shard, "fsdp", axis=0, tiled=True)
            for shard in (w_qkv, w_out, w_cross_q, w_cross_kv, w_cross_out, w_fc_in, w_fc_out)
        )
    seq_count, row_count, model_width = latents.shape
    flat_rows = seq_count * row_count
    text_rows = captions.shape[1]
    modulation = full_table.astype(jnp.float32)[None] + conditions.reshape(
        seq_count, 6, model_width
    )
    shift_one, scale_one, gate_one, shift_two, scale_two, gate_two = jnp.moveaxis(modulation, 1, 0)
    residual_in = latents.astype(jnp.float32)
    normed_one, pull_one = jax.vjp(modulate, residual_in, shift_one, scale_one)
    normed_low = normed_one.astype(jnp.bfloat16).reshape(flat_rows, model_width)
    joined = (
        product(normed_low, full_qkv)
        .astype(jnp.bfloat16)
        .reshape(seq_count, row_count, 3 * model_width)
    )
    queries = joined[..., :model_width]
    own_kv = joined[..., model_width:]
    if whole_tiles:
        all_kv = jnp.moveaxis(exchange_gather(own_kv, "seq"), 0, 1).reshape(
            seq_count, -1, 2 * model_width
        )
    else:
        all_kv = lax.all_gather(own_kv, "seq", axis=1, tiled=True)
    all_keys = all_kv[..., :model_width]
    all_values = all_kv[..., model_width:]
    mixed_self, log_self = attention_forward(queries, all_keys, all_values)
    branch = product(mixed_self.reshape(flat_rows, model_width), full_out).reshape(
        seq_count, row_count, model_width
    )
    after_self = residual_in + gate_one[:, None] * branch
    cross_in = after_self.astype(jnp.bfloat16).reshape(flat_rows, model_width)
    cross_query = (
        product(cross_in, full_cq).astype(jnp.bfloat16).reshape(seq_count, row_count, model_width)
    )
    caption_rows = captions.reshape(seq_count * text_rows, model_width)
    cross_kv = (
        product(caption_rows, full_ckv)
        .astype(jnp.bfloat16)
        .reshape(seq_count, text_rows, 2 * model_width)
    )
    cross_keys = cross_kv[..., :model_width]
    cross_values = cross_kv[..., model_width:]
    cross_mixed, log_cross = attention_forward(cross_query, cross_keys, cross_values)
    cross_flat = cross_mixed.reshape(flat_rows, model_width)
    after_cross = after_self + product(cross_flat, full_co).reshape(
        seq_count, row_count, model_width
    )
    normed_two, pull_two = jax.vjp(modulate, after_cross, shift_two, scale_two)
    normed_two_low = normed_two.astype(jnp.bfloat16).reshape(flat_rows, model_width)
    hidden_pre = product(normed_two_low, full_fc_in)
    hidden, pull_gelu = jax.vjp(gelu_tanh, hidden_pre)
    hidden_low = hidden.astype(jnp.bfloat16)
    expanded = product(hidden_low, full_fc_out).reshape(seq_count, row_count, model_width)
    output = (after_cross + gate_two[:, None] * expanded).astype(jnp.bfloat16)
    back_qkv, back_out, back_cq, back_ckv = full_qkv, full_out, full_cq, full_ckv
    back_co, back_fc_in, back_fc_out = full_co, full_fc_in, full_fc_out
    grad_out = cotangent.astype(jnp.float32)
    grad_gate_two = jnp.sum(grad_out * expanded, axis=1)
    grad_expanded = (
        (grad_out * gate_two[:, None]).astype(jnp.bfloat16).reshape(flat_rows, model_width)
    )
    grad_fc_out = outer_sum(hidden_low, grad_expanded)
    grad_hidden = back_product(grad_expanded, back_fc_out)
    grad_pre = pull_gelu(grad_hidden)[0].astype(jnp.bfloat16)
    grad_fc_in = outer_sum(normed_two_low, grad_pre)
    grad_normed_two = back_product(grad_pre, back_fc_in).reshape(seq_count, row_count, model_width)
    grad_cross_side, grad_shift_two, grad_scale_two = pull_two(grad_normed_two)
    grad_after_cross = grad_out + grad_cross_side
    grad_cross_branch = grad_after_cross.astype(jnp.bfloat16).reshape(flat_rows, model_width)
    grad_cross_out = outer_sum(cross_flat, grad_cross_branch)
    grad_cross_mixed = (
        back_product(grad_cross_branch, back_co)
        .astype(jnp.bfloat16)
        .reshape(seq_count, row_count, model_width)
    )
    grad_cq_rows, grad_cross_keys, grad_cross_values = attention_backward(
        cross_query, cross_keys, cross_values, log_cross, grad_cross_mixed
    )
    grad_cross_query = grad_cq_rows.astype(jnp.bfloat16).reshape(flat_rows, model_width)
    grad_cross_q = outer_sum(cross_in, grad_cross_query)
    grad_after_self = grad_after_cross + back_product(grad_cross_query, back_cq).reshape(
        seq_count, row_count, model_width
    )
    grad_cross_part = jnp.concatenate([grad_cross_keys, grad_cross_values], axis=-1)
    grad_gate_one = jnp.sum(grad_after_self * branch, axis=1)
    grad_branch = (
        (grad_after_self * gate_one[:, None]).astype(jnp.bfloat16).reshape(flat_rows, model_width)
    )
    grad_w_out = outer_sum(mixed_self.reshape(flat_rows, model_width), grad_branch)
    grad_mixed = (
        back_product(grad_branch, back_out)
        .astype(jnp.bfloat16)
        .reshape(seq_count, row_count, model_width)
    )
    grad_queries, grad_keys, grad_values = attention_backward(
        queries, all_keys, all_values, log_self, grad_mixed
    )
    grad_keys_own, grad_values_own = (
        exchange_sum_scatter(
            grad.astype(jnp.bfloat16).reshape(seq_count, -1, row_count, model_width), "seq", lead=1
        )
        for grad in (grad_keys, grad_values)
    )
    grad_joined = (
        jnp.concatenate([grad_queries, grad_keys_own, grad_values_own], axis=-1)
        .astype(jnp.bfloat16)
        .reshape(flat_rows, 3 * model_width)
    )
    grad_w_qkv = outer_sum(normed_low, grad_joined)
    grad_normed_one = back_product(grad_joined, back_qkv).reshape(seq_count, row_count, model_width)
    grad_in_side, grad_shift_one, grad_scale_one = pull_one(grad_normed_one)
    grad_latents = grad_after_self + grad_in_side
    grad_modulation = jnp.stack(
        [
            grad_shift_one,
            grad_scale_one,
            grad_gate_one,
            grad_shift_two,
            grad_scale_two,
            grad_gate_two,
        ],
        axis=1,
    )
    summed_cross = exchange_sum(grad_cross_part, "seq")
    summed_mod = exchange_sum(grad_modulation, "seq")
    grad_cross_low = summed_cross.astype(jnp.bfloat16).reshape(
        seq_count * text_rows, 2 * model_width
    )
    grad_cross_kv = outer_sum(caption_rows, grad_cross_low)
    grad_captions = back_product(grad_cross_low, back_ckv).reshape(
        seq_count, text_rows, model_width
    )
    grad_conditions = summed_mod.reshape(seq_count, 6 * model_width)
    grad_mlp_shift = summed_mod[:, 3]
    grad_table_full = jnp.sum(summed_mod, axis=0)
    table_rows = jnp.moveaxis(grad_table_full.reshape(6, lax.axis_size("fsdp"), -1), 1, 0)
    owned_table = exchange_sum_scatter(table_rows, "fsdp")
    if whole_tiles:
        first_of_seq = (lax.axis_index("seq") == 0).astype(jnp.float32)
        fc_out_blocks = grad_fc_out.astype(jnp.bfloat16).reshape(
            lax.axis_size("fsdp"), -1, rows, width
        )
        owned = in_groups(
            scatter_units,
            [fc_out_blocks[:, i] for i in range(fc_out_blocks.shape[1])]
            + grad_units(grad_fc_in)
            + grad_units(grad_cross_out)
            + grad_units(grad_cross_q)
            + grad_units(grad_cross_kv * first_of_seq)
            + grad_units(grad_w_out)
            + grad_units(grad_w_qkv),
        )
        owned_fc_out = jnp.concatenate(owned[0:4], axis=0)
        owned_fc_in = jnp.concatenate(owned[4:8], axis=1)
        owned_co, owned_cq = owned[8], owned[9]
        owned_kv_cross = jnp.concatenate(owned[10:12], axis=1)
        owned_out = owned[12]
        owned_qkv = jnp.concatenate(owned[13:16], axis=1)
    else:
        column_parts = (
            lax.psum_scatter(grad_w_qkv.astype(jnp.bfloat16), "seq", scatter_dimension=1, tiled=True),
            lax.psum_scatter(grad_w_out.astype(jnp.bfloat16), "seq", scatter_dimension=1, tiled=True),
            lax.psum_scatter(grad_cross_q.astype(jnp.bfloat16), "seq", scatter_dimension=1, tiled=True),
            lax.psum_scatter(grad_cross_out.astype(jnp.bfloat16), "seq", scatter_dimension=1, tiled=True),
            lax.psum_scatter(grad_fc_in.astype(jnp.bfloat16), "seq", scatter_dimension=1, tiled=True),
            lax.psum_scatter(grad_fc_out.astype(jnp.bfloat16), "seq", scatter_dimension=1, tiled=True),
        )
        owned_parts = (
            lax.psum_scatter(grad_cross_kv.astype(jnp.bfloat16), "fsdp", scatter_dimension=0, tiled=True),
            lax.psum_scatter(column_parts[0], "fsdp", scatter_dimension=0, tiled=True),
            lax.psum_scatter(column_parts[1], "fsdp", scatter_dimension=0, tiled=True),
            lax.psum_scatter(column_parts[2], "fsdp", scatter_dimension=0, tiled=True),
            lax.psum_scatter(column_parts[3], "fsdp", scatter_dimension=0, tiled=True),
            lax.psum_scatter(column_parts[4], "fsdp", scatter_dimension=0, tiled=True),
            lax.psum_scatter(column_parts[5], "fsdp", scatter_dimension=0, tiled=True),
        )
        owned_kv_cross = owned_parts[0].astype(jnp.float32)
        owned_qkv, owned_out, owned_cq, owned_co, owned_fc_in, owned_fc_out = (
            lax.all_gather(owned_parts[1], "seq", axis=1, tiled=True).astype(jnp.float32),
            lax.all_gather(owned_parts[2], "seq", axis=1, tiled=True).astype(jnp.float32),
            lax.all_gather(owned_parts[3], "seq", axis=1, tiled=True).astype(jnp.float32),
            lax.all_gather(owned_parts[4], "seq", axis=1, tiled=True).astype(jnp.float32),
            lax.all_gather(owned_parts[5], "seq", axis=1, tiled=True).astype(jnp.float32),
            lax.all_gather(owned_parts[6], "seq", axis=1, tiled=True).astype(jnp.float32),
        )
    return (
        output,
        grad_latents,
        grad_captions,
        grad_conditions,
        grad_mlp_shift,
        owned_table,
        owned_qkv,
        owned_out,
        owned_cq,
        owned_kv_cross,
        owned_co,
        owned_fc_in,
        owned_fc_out,
    )


def solution(mesh):
    in_specs = (
        P("fsdp", "seq", None),
        P("fsdp", None, None),
        P("fsdp", None),
        P(None, "fsdp"),
        P("fsdp", None),
        P("fsdp", None),
        P("fsdp", None),
        P("fsdp", None),
        P("fsdp", None),
        P("fsdp", None),
        P("fsdp", None),
        P("fsdp", "seq", None),
    )
    out_specs = (
        P("fsdp", "seq", None),
        P("fsdp", "seq", None),
        P("fsdp", None, None),
        P("fsdp", None),
        P("fsdp", None),
        P(None, "fsdp"),
        P("fsdp", None),
        P("fsdp", None),
        P("fsdp", None),
        P("fsdp", None),
        P("fsdp", None),
        P("fsdp", None),
        P("fsdp", None),
    )
    return jax.shard_map(body, mesh=mesh, in_specs=in_specs, out_specs=out_specs, check_vma=False)
```
